512 devices in a mesh: tm: 64 (over z, x_hi, core), rows: 8 (over x_lo, y).
Axes of the slice: x: 4 (x_hi: 2, x_lo: 2; x = x_hi * 2 + x_lo), y: 4, z: 16, core: 2. Of those that a mesh axis runs over, the one named last changes fastest.
Arguments:
- right_side: float32 [192, 16384], P('tm'), as said below
- aux_field: float32 [192, 16384], P('tm'), may hold values from -0.3 to 0.3
- hopping: float32 [16384, 16384], P('rows', 'tm'), as said below
Outputs:
- solution: float32 [192, 16384], P('tm')
- residual: float32 [192, 16384], P('tm')
The draws below stay inside these ranges and needn't reach their ends.
Inputs may be any that keep to these rules, and one draw needn't show every extreme that they name: `right_side`: float entries, no structure promised. `hopping`: dense float entries, no structure promised.
All inputs are finite; a program needn't handle non-finite values.
Results may differ from the reference program's by a relative error of at most 0.00028.
Values sent between devices are 32-bit elements; how exact they have to be, the bound alone decides.
A program may use at most 64 MiB of HBM per device.

```python
import math
import jax
import jax.numpy as jnp
from jax import lax

N = 16384
ITERS = 2
NT = 192


def draw_right_side(key, part):
    key = jax.random.fold_in(key, 1)
    position = lax.broadcasted_iota(jnp.float32, (NT, N), 0) / (NT - 1)
    values = jax.random.truncated_normal(key, -4.0, 4.0, (NT, N), jnp.float32)
    return values * jnp.exp(position * math.log(3.0))


def draw_hopping(key, part):
    key = jax.random.fold_in(key, 2)
    noise = jax.random.normal(key, (N, N), jnp.float32)
    row_ids = lax.broadcasted_iota(jnp.int32, (N, 1), 0)
    col_ids = lax.broadcasted_iota(jnp.int32, (1, N), 1)
    diagonal = (row_ids == col_ids).astype(jnp.float32)
    return 0.45 * diagonal + noise * (0.15 / math.sqrt(N))


def block_scale(own_key, extent, split, smallest, high):
    def one(dim, parts):
        steps = jax.random.uniform(jax.random.fold_in(jax.random.fold_in(own_key, 6), dim), (parts,), jnp.float32, smallest / len(split), high / len(split))
        return jnp.repeat(jnp.exp(steps), extent[dim] // parts).reshape((-1,) + (1,) * (len(extent) - dim - 1))

    factor_of = one(*split[0])
    for cut in split[1:]:
        factor_of = factor_of * one(*cut)
    return factor_of


def setup_inputs(seed: int = 0) -> dict:
    arg_keys = jax.random.split(jax.random.key(seed), 4)
    return {
        "right_side": draw_right_side(jax.random.fold_in(arg_keys[3], 71), 0),
        "aux_field": jnp.clip(jax.random.uniform(arg_keys[1], (NT, N), jnp.float32, -0.3, 0.3) * block_scale(arg_keys[1], (NT, N), ((0, 64),), -0.4, 0.0), -0.3, 0.3),
        "hopping": draw_hopping(jax.random.fold_in(arg_keys[3], 71), 0),
    }


def forward(vector, aux_field, hopping):
    previous = jnp.concatenate([-vector[-1:], vector[:-1]], axis=0)
    hopped = lax.dot_general(previous, hopping, (((1,), (1,)), ((), ())), precision=lax.Precision.HIGHEST, preferred_element_type=jnp.float32)
    return vector - jnp.exp(aux_field) * hopped


def backward(mapped, aux_field, hopping):
    weighted = jnp.exp(aux_field) * mapped
    following = jnp.concatenate([weighted[1:], -weighted[:1]], axis=0)
    return mapped - jnp.dot(following, hopping, precision=lax.Precision.HIGHEST, preferred_element_type=jnp.float32)


def reference(right_side, aux_field, hopping):
    solution = jnp.zeros_like(right_side)
    residual = right_side
    direction = right_side
    norm_now = jnp.sum(residual * residual)
    for iteration in range(ITERS):
        image = backward(forward(direction, aux_field, hopping), aux_field, hopping)
        step_size = norm_now / jnp.sum(direction * image)
        solution = solution + step_size * direction
        residual = residual - step_size * image
        norm_next = jnp.sum(residual * residual)
        direction = residual + (norm_next / norm_now) * direction
        norm_now = norm_next
    return solution, residual
```

```python
import functools

import jax
import jax.numpy as jnp
from jax import lax
from jax.experimental import pallas as pl
from jax.experimental.pallas import tpu as pltpu
from jax.sharding import PartitionSpec as P

SR = 8
F32 = jnp.float32
BF16 = jnp.bfloat16


def split(value):
    high = value.astype(BF16)
    return high, (value - high.astype(F32)).astype(BF16)


def product(a_high, a_low, b_high, b_low):
    dot = functools.partial(jnp.dot, preferred_element_type=F32)
    return dot(a_high, b_high) + (dot(a_low, b_high) + dot(a_high, b_low))


def fold(value, width):
    squared = value * value
    rows = squared.shape[0]
    tile = squared.reshape(rows // SR, SR, squared.shape[1]).sum(axis=0)
    out = tile[:, :width]
    for start in range(width, squared.shape[1], width):
        out = out + tile[:, start : start + width]
    return out


def total(tile):
    return jnp.sum(jnp.sum(tile, axis=0, keepdims=True), axis=1, keepdims=True)


def arrived(ref, sem):
    pltpu.make_async_copy(ref, ref, sem).wait()


def kernel(
    tm, rows, b_ref, aux_ref, h_ref, x_out, r_out,
    hf_hi, hf_lo, hb_hi, hb_lo,
    b_in, aux_in, b_piece, r_piece, e_send, einv_send, e_mid, e_diag,
    v_full, v_hi, v_lo, v_fold, part, sib_in, right_in, left_in, x_buf, x_in,
    q_mid, gath, acc, c_acc, rs_send, rs_in, out_send, out_mid,
    b_sem, aux_sem, ag_sem, emid_sem, ediag_sem,
    fsib_sem, fr_sem, fl_sem, fx_sem, br_sem, bl_sem, bsib_sem, rs_sem,
    tr_sem, fin_sem, init_send, ag_send, emid_send, ediag_send,
    fsib_send, fr_send, fl_send, fx_send, br_send, bl_send, bsib_send, rs_send_sem,
    tr_send, fin_send, loc_sem,
):
    m = lax.axis_index("tm")
    r = lax.axis_index("rows")
    z = m // 4
    core = m % 2
    other = 1 - core
    nz = tm // 4
    nr, nl = nz // 2, nz // 2 - 1
    g = tm // rows
    steps = b_ref.shape[0]
    t_all = steps * tm
    tg, ht = t_all // rows, t_all // 2
    cw = h_ref.shape[1]
    rw = h_ref.shape[0]
    w = rw // nz
    zper = cw // w
    half_rows = rows // 2
    is_diag = r == m // g

    sibling = (m + 1 - 2 * core, r)
    x_other = (m + 2 - 4 * ((m // 2) % 2), r)
    right = (lax.rem(m + 4, tm), r)
    left = (lax.rem(m + tm - 4, tm), r)

    def send(src, dst, ssem, rsem, device):
        pltpu.make_async_remote_copy(
            src_ref=src, dst_ref=dst, send_sem=ssem, recv_sem=rsem,
            device_id=device, device_id_type=pl.DeviceIdType.MESH,
        ).start()

    nxt = lax.rem(r + 1, rows)
    mine = lax.rem(m, g)
    for k in range(g):
        target = (nxt * g + k, m // g)
        cols = pl.ds(pl.multiple_of((nxt * g + k) * cw, cw), cw)
        send(b_ref.at[:, cols], b_in.at[mine], init_send.at[0, k], b_sem.at[mine], target)
    for k in range(g):
        target = (nxt * g + k, m // g)
        cols = pl.ds(pl.multiple_of((nxt * g + k) * cw, cw), cw)
        send(aux_ref.at[:, cols], aux_in.at[mine], init_send.at[1, k], aux_sem.at[mine], target)

    def prepare(chunk, carry):
        block = h_ref[pl.ds(pl.multiple_of(chunk * w, w), w), :]
        high, low = split(block)
        hb_hi[chunk] = high
        hb_lo[chunk] = low
        high, low = split(block.T)
        hf_hi[chunk] = high
        hf_lo[chunk] = low
        return carry

    lax.fori_loop(0, nz, prepare, 0)

    def spread(source, it):
        for d in range(1, rows):
            send(source, v_full.at[it, r], ag_send.at[it], ag_sem.at[it], (m, lax.rem(r + d, rows)))

    for i in range(g):
        arrived(b_in.at[i], b_sem.at[i])
        b_piece[steps * i : steps * (i + 1), :] = b_in[i]
    spread(b_piece, 0)
    v_full[0, r] = b_piece[...]

    for i in range(g):
        arrived(aux_in.at[i], aux_sem.at[i])
        value = aux_in[i]
        einv_send[steps * i : steps * (i + 1), :] = jnp.exp(-value)
        grown = jnp.exp(value)
        for h in range(zper):
            e_send[h, steps * i : steps * (i + 1), :] = grown[:, h * w : (h + 1) * w]

    for h in range(zper):
        for xh in range(2):
            to_m = (zper * mine + h) * 4 + xh * 2 + r // half_rows
            to_r = m // g
            same = jnp.logical_and(to_m == m, to_r == r)
            sem = emid_sem.at[lax.rem(r, half_rows)]

            @pl.when(same)
            def _():
                pltpu.make_async_copy(e_send.at[h], e_mid.at[lax.rem(r, half_rows)], sem).start()

            @pl.when(jnp.logical_not(same))
            def _():
                send(e_send.at[h], e_mid.at[lax.rem(r, half_rows)], emid_send.at[h, xh], sem, (to_m, to_r))

    @pl.when(is_diag)
    def _():
        e_diag[r] = einv_send[...]

    @pl.when(jnp.logical_not(is_diag))
    def _():
        send(einv_send, e_diag.at[r], ediag_send.at[0], ediag_sem.at[0], (m, m // g))

    row_id = lax.broadcasted_iota(jnp.int32, (t_all, 1), 0)

    def forward(it):
        v = v_full[it].reshape(t_all, cw)
        shifted = pltpu.roll(v, 1, 0)
        shifted = jnp.where(row_id == 0, -shifted, shifted)
        high, low = split(shifted)
        v_hi[...] = high
        v_lo[...] = low
        squares = fold(v, w)

        @pl.when(is_diag)
        def _():
            if it == 0:
                arrived(e_diag.at[pl.ds(0, rows - 1)], ediag_sem.at[0])
            inverse = e_diag[...].reshape(t_all, cw) * v
            for h in range(zper):
                v_fold[h] = inverse[:, h * w : (h + 1) * w]

        def compute(k):
            chunk = lax.rem(z + k, nz)
            value = product(v_hi[...], v_lo[...], hf_hi[chunk], hf_lo[chunk])
            part[it, k, 0, :ht, :] = value[:ht]
            part[it, k, 1, :ht, :] = value[ht:]
            part[it, k, 0, ht:, :] = squares
            part[it, k, 1, ht:, :] = squares

            @pl.when(jnp.logical_and(is_diag, chunk // zper == mine))
            def _():
                own = v_fold[lax.rem(chunk, zper)]
                part[it, k, 0, :ht, :] -= own[:ht]
                part[it, k, 1, :ht, :] -= own[ht:]

            send(part.at[it, k, other], sib_in.at[it, k], fsib_send.at[it], fsib_sem.at[it, k], sibling)

        compute(nr)
        compute(nr + 1)

        def step(s, carry):
            @pl.when(s < nr)
            def _():
                compute(nr - s)
                compute(lax.rem(nr + 1 + s, nz))

            k = nr + 1 - s
            arrived(sib_in.at[it, k], fsib_sem.at[it, k])
            part[it, k, core] += sib_in[it, k]

            @pl.when(s > 1)
            def _():
                arrived(right_in.at[it, s - 2], fr_sem.at[it, s - 2])
                part[it, k, core] += right_in[it, s - 2]

            send(part.at[it, k, core], right_in.at[it, s - 1], fr_send.at[it], fr_sem.at[it, s - 1], right)

            @pl.when(s <= nl)
            def _():
                k = nr + s
                arrived(sib_in.at[it, k], fsib_sem.at[it, k])
                part[it, k, core] += sib_in[it, k]

                @pl.when(s > 1)
                def _():
                    arrived(left_in.at[it, s - 2], fl_sem.at[it, s - 2])
                    part[it, k, core] += left_in[it, s - 2]

                send(part.at[it, k, core], left_in.at[it, s - 1], fl_send.at[it], fl_sem.at[it, s - 1], left)

            return carry

        lax.fori_loop(1, nr + 1, step, 0)
        arrived(sib_in.at[it, 0], fsib_sem.at[it, 0])
        arrived(left_in.at[it, nl - 1], fl_sem.at[it, nl - 1])
        arrived(right_in.at[it, nr - 1], fr_sem.at[it, nr - 1])
        own = part[it, 0, core] + sib_in[it, 0] + (left_in[it, nl - 1] + right_in[it, nr - 1])
        x_buf[it] = own
        send(x_buf.at[it], x_in.at[it], fx_send.at[it], fx_sem.at[it], x_other)
        arrived(x_in.at[it], fx_sem.at[it])
        summed = own + x_in[it]
        return summed[:ht], total(summed[ht:])

    def backward(it, q, e):
        gath[it, 0, core, :ht, :] = e * q
        gath[it, 0, core, ht:, :] = fold(q, w)

        def to_sibling(k):
            send(gath.at[it, k, core], gath.at[it, k, core], bsib_send.at[it], bsib_sem.at[it, k], sibling)

        def to_right(k, s):
            send(gath.at[it, k, core], gath.at[it, lax.rem(k + nz - 1, nz), core],
                 br_send.at[it], br_sem.at[it, s], right)

        def to_left(k, s):
            send(gath.at[it, k, core], gath.at[it, k + 1, core], bl_send.at[it], bl_sem.at[it, s], left)

        to_right(0, 0)
        to_left(0, 0)
        to_sibling(0)
        acc[...] = jnp.zeros_like(acc)
        c_acc[...] = jnp.zeros_like(c_acc)

        def use(k):
            arrived(gath.at[it, k, other], bsib_sem.at[it, k])
            block = jnp.concatenate([gath[it, k, 0, :ht, :], gath[it, k, 1, :ht, :]], axis=0)
            high, low = split(block)
            chunk = lax.rem(z + k, nz)
            acc[...] += product(high, low, hb_hi[chunk], hb_lo[chunk])
            c_acc[...] += gath[it, k, 0, ht:, :] + gath[it, k, 1, ht:, :]

        def step(s, carry):
            k = nz - s
            arrived(gath.at[it, k, core], br_sem.at[it, s - 1])

            @pl.when(s < nr)
            def _():
                to_right(k, s)

            to_sibling(k)

            @pl.when(s <= nl)
            def _():
                arrived(gath.at[it, s, core], bl_sem.at[it, s - 1])

                @pl.when(s < nl)
                def _():
                    to_left(s, s)

                to_sibling(s)

            use(lax.rem(nz - s + 1, nz))

            @pl.when(s > 1)
            def _():
                use(s - 1)

            return carry

        lax.fori_loop(1, nr + 1, step, 0)
        use(nz // 2)

        returned = pltpu.roll(acc[...], t_all - 1, 0)
        acc[...] = jnp.where(row_id == t_all - 1, returned, -returned)

        @pl.when(is_diag)
        def _():
            for h in range(zper):
                k = lax.rem(zper * mine + h + nz - z, nz)
                block = jnp.concatenate([gath[it, k, 0, :ht, :], gath[it, k, 1, :ht, :]], axis=0)
                inverse = e_diag[:, :, h * w : (h + 1) * w].reshape(t_all, w)
                acc[:, h * w : (h + 1) * w] += inverse * block

        for k in range(rows):
            for h in range(zper):
                rs_send[it, k, h * tg : (h + 1) * tg, :] = acc[k * tg : (k + 1) * tg, h * w : (h + 1) * w]
            rs_send[it, k, zper * tg :, :] = c_acc[...]
        for d in range(1, rows):
            to = lax.rem(r + d, rows)
            send(rs_send.at[it, to], rs_in.at[it, r], rs_send_sem.at[it], rs_sem.at[it], (m, to))
        rs_in[it, r] = rs_send[it, r]
        arrived(rs_send.at[it, pl.ds(0, rows - 1)], rs_sem.at[it])
        summed = rs_in[it, 0]
        for k in range(1, rows):
            summed = summed + rs_in[it, k]
        image = jnp.concatenate([summed[h * tg : (h + 1) * tg] for h in range(zper)], axis=1)
        return image, total(summed[zper * tg :])

    arrived(v_full.at[0, pl.ds(0, rows - 1)], ag_sem.at[0])
    summed, norm_0 = forward(0)
    for i in range(half_rows):
        arrived(e_mid.at[i], emid_sem.at[i])
    e = e_mid[...].reshape(ht, w)
    q = -(e * summed)
    q_mid[...] = q
    image, curvature = backward(0, q, e)
    step_0 = norm_0 / curvature
    residual = b_piece[...] - step_0 * image
    r_piece[...] = residual
    spread(r_piece, 1)
    v_full[1, r] = residual
    arrived(v_full.at[1, pl.ds(0, rows - 1)], ag_sem.at[1])

    summed, norm_1 = forward(1)
    beta = norm_1 / norm_0
    e = e_mid[...].reshape(ht, w)
    q = beta * q_mid[...] - e * summed
    image, curvature = backward(1, q, e)
    step_1 = norm_1 / curvature
    b = b_piece[...]
    residual = r_piece[...]
    answer = step_0 * b + step_1 * (residual + beta * b)
    residual = residual - step_1 * image

    for i in range(g):
        out_send[i, 0] = answer[steps * i : steps * (i + 1)]
        out_send[i, 1] = residual[steps * i : steps * (i + 1)]
    to_row = lax.rem(m // g + rows - 1, rows)
    for i in range(g):
        send(out_send.at[i], out_mid.at[mine], tr_send.at[i], tr_sem.at[mine], (g * r + i, to_row))
    for k in range(g):
        arrived(out_mid.at[k], tr_sem.at[k])
    here = pl.multiple_of(nxt * rw, rw)
    for k in range(g):
        x_out[:, pl.ds(here + k * cw, cw)] = out_mid[k, 0]
        r_out[:, pl.ds(here + k * cw, cw)] = out_mid[k, 1]
    block = pl.ds(here, rw)
    for d in range(1, rows):
        to = (m, lax.rem(r + d, rows))
        send(x_out.at[:, block], x_out.at[:, block], fin_send.at[0, d - 1], fin_sem.at[0, d - 1], to)
        send(r_out.at[:, block], r_out.at[:, block], fin_send.at[1, d - 1], fin_sem.at[1, d - 1], to)
    for d in range(1, rows):
        source = lax.rem(r + rows - d, rows)
        there = pl.ds(pl.multiple_of(lax.rem(source + 1, rows) * rw, rw), rw)
        arrived(x_out.at[:, there], fin_sem.at[0, d - 1])
        arrived(r_out.at[:, there], fin_sem.at[1, d - 1])

    for d in range(1, rows):
        arrived(x_out.at[:, block], fin_send.at[0, d - 1])
        arrived(r_out.at[:, block], fin_send.at[1, d - 1])
    for i in range(g):
        arrived(out_send.at[i], tr_send.at[i])
        arrived(b_in.at[i], init_send.at[0, i])
        arrived(aux_in.at[i], init_send.at[1, i])
    for h in range(zper):
        for xh in range(2):
            to_m = (zper * mine + h) * 4 + xh * 2 + r // half_rows
            same = jnp.logical_and(to_m == m, m // g == r)

            @pl.when(jnp.logical_not(same))
            def _():
                arrived(e_send.at[h], emid_send.at[h, xh])

    @pl.when(jnp.logical_not(is_diag))
    def _():
        arrived(einv_send, ediag_send.at[0])

    for it in range(2):
        arrived(v_full.at[it, pl.ds(0, rows - 1)], ag_send.at[it])
        arrived(sib_in.at[it], fsib_send.at[it])
        arrived(right_in.at[it], fr_send.at[it])
        arrived(left_in.at[it], fl_send.at[it])
        arrived(x_in.at[it], fx_send.at[it])
        arrived(right_in.at[it], br_send.at[it])
        arrived(left_in.at[it], bl_send.at[it])
        arrived(sib_in.at[it], bsib_send.at[it])
        arrived(rs_send.at[it, pl.ds(0, rows - 1)], rs_send_sem.at[it])


def per_device(tm, rows, right_side, aux_field, hopping):
    steps = right_side.shape[0]
    t_all = steps * tm
    tg, ht = t_all // rows, t_all // 2
    rw, cw = hopping.shape
    nz = tm // 4
    nr, nl = nz // 2, nz // 2 - 1
    g = tm // rows
    w = rw // nz
    zper = cw // w
    vm = pltpu.VMEM
    dma = pltpu.SemaphoreType.DMA
    scratch = [
        vm((nz, cw, w), BF16), vm((nz, cw, w), BF16), vm((nz, w, cw), BF16), vm((nz, w, cw), BF16),
        vm((g, steps, cw), F32), vm((g, steps, cw), F32), vm((tg, cw), F32), vm((tg, cw), F32),
        vm((zper, tg, w), F32), vm((tg, cw), F32), vm((rows // 2, tg, w), F32), vm((rows, tg, cw), F32),
        vm((2, rows, tg, cw), F32), vm((t_all, cw), BF16), vm((t_all, cw), BF16), vm((zper, t_all, w), F32),
        vm((2, nz, 2, ht + SR, w), F32), vm((2, nz, ht + SR, w), F32),
        vm((2, nr, ht + SR, w), F32), vm((2, nl, ht + SR, w), F32),
        vm((2, ht + SR, w), F32), vm((2, ht + SR, w), F32),
        vm((ht, w), F32), vm((2, nz, 2, ht + SR, w), F32), vm((t_all, cw), F32), vm((SR, w), F32),
        vm((2, rows, zper * tg + SR, w), F32), vm((2, rows, zper * tg + SR, w), F32),
        vm((g, 2, steps, cw), F32), vm((g, 2, steps, cw), F32),
        dma((g,)), dma((g,)), dma((2,)), dma((rows // 2,)), dma((1,)),
        dma((2, nz)), dma((2, nr)), dma((2, nl)), dma((2,)),
        dma((2, nr)), dma((2, nl)), dma((2, nz)), dma((2,)),
        dma((g,)), dma((2, rows)), dma((2, g)), dma((2,)), dma((zper, 2)), dma((1,)),
        dma((2,)), dma((2,)), dma((2,)), dma((2,)), dma((2,)), dma((2,)), dma((2,)), dma((2,)),
        dma((g,)), dma((2, rows)), dma((1,)),
    ]
    out = jax.ShapeDtypeStruct(right_side.shape, F32)
    in_vmem = pl.BlockSpec(memory_space=pltpu.VMEM)
    return pl.pallas_call(
        functools.partial(kernel, tm, rows),
        out_shape=(out, out),
        in_specs=[in_vmem] * 3,
        out_specs=(in_vmem, in_vmem),
        scratch_shapes=scratch,
        compiler_params=pltpu.CompilerParams(has_side_effects=True, vmem_limit_bytes=48 * 1024 * 1024),
        cost_estimate=pl.CostEstimate(
            flops=24 * t_all * rw * cw, bytes_accessed=4 * rw * cw, transcendentals=2 * tg * cw
        ),
    )(right_side, aux_field, hopping)


def solution(mesh):
    in_specs = (P("tm", None), P("tm", None), P("rows", "tm"))
    out_specs = (P("tm", None), P("tm", None))
    call = functools.partial(per_device, mesh.shape["tm"], mesh.shape["rows"])
    return jax.shard_map(call, mesh=mesh, in_specs=in_specs, out_specs=out_specs, check_vma=False)
```
